32 devices in a mesh: seq: 4 (over x, core), head: 4 (over z), batch: 2 (over y).
Axes of the slice: x: 2, y: 2, z: 4, core: 2. Of those that a mesh axis runs over, the one named last changes fastest.
Arguments:
- hyena_inputs: bfloat16 [4096, 3, 8192], P(('batch', 'seq'), None, 'head'), parts along dimension 0, may hold values from -6 to 6
- short_filter: float32 [3, 3, 8192], P(None, None, 'head'), may hold values from -3.5 to 3.5
- medium_filter: float32 [128, 8192], P(None, 'head'), may hold values from -0.5 to 0.5
- q_proj: bfloat16 [4096, 8192], P(('batch', 'seq'), 'head'), parts along dimension 0, may hold values from -8 to 8
- k_proj: bfloat16 [4096, 8192], P(('batch', 'seq'), 'head'), parts along dimension 0, may hold values from -8 to 8
- out_weight: bfloat16 [8192, 8192], P('head'), may hold values from -0.25 to 0.25
Outputs:
- hyena_out: bfloat16 [4096, 8192], P(('batch', 'seq'), 'head'), parts along dimension 0
- mixed: bfloat16 [4096, 8192], P(('batch', 'seq'), 'head'), parts along dimension 0
The draws below stay inside these ranges and needn't reach their ends.
There are 2 independent parts, one for each index of `batch`. The reference program is written for one: setup_inputs(seed, part) draws one part's arguments, and reference() takes and returns one part's arrays. A program takes and returns all parts, laid end to end along the dimension named above; an argument that names none is the same for every part. Nothing has to cross between parts.
All inputs are finite; a program needn't handle non-finite values.
Results may differ from the reference program's by a relative error of at most 0.011.
Values may be sent and summed in bfloat16 or wider, within the bound.
A program may use at most 192 MiB of HBM per device.

```python
import jax
import jax.numpy as jnp
from jax import lax

D = 8192
HEAD_SIZE = 128
SHORT = 3
MED = 128
LEN = 2048
N_HEAD = 4


def paired_draw(key):
    seeded = jax.random.fold_in(key, 4051)
    key_query, key_keys = jax.random.split(seeded, 2)
    queries = jnp.clip(1.5 * jax.random.normal(key_query, (LEN, D), jnp.float32), -8.0, 8.0)
    keys = jnp.clip(1.5 * jax.random.normal(key_keys, (LEN, D), jnp.float32), -8.0, 8.0)
    return (queries, keys)


def draw_q_proj(key, part):
    return paired_draw(key)[0].astype(jnp.bfloat16)


def draw_k_proj(key, part):
    return paired_draw(key)[1].astype(jnp.bfloat16)


def block_levels(stream_key, dims, cuts, smallest, largest):
    def one(axis_at, blocks):
        heights = jax.random.uniform(jax.random.fold_in(jax.random.fold_in(stream_key, 6), axis_at), (blocks,), jnp.float32, smallest / len(cuts), largest / len(cuts))
        return jnp.repeat(jnp.exp(heights), dims[axis_at] // blocks).reshape((-1,) + (1,) * (len(dims) - axis_at - 1))

    level = one(*cuts[0])
    for cut in cuts[1:]:
        level = level * one(*cut)
    return level


def normal_values(key, dims, scale, reach, pieces=(), kind=jnp.bfloat16):
    values = jax.random.normal(key, dims, jnp.float32) * scale
    if len(pieces) > 0:
        values = block_levels(key, dims, pieces, -0.22, 0.18) * values
    return jnp.clip(values, min=-reach, max=reach).astype(kind)


def setup_inputs(seed: int = 0, part: int = 0) -> dict:
    key_of = jax.random.split(jax.random.key(seed), 7)
    part_keys = jax.random.split(jax.random.fold_in(key_of[6], part), 7)
    return {
        "hyena_inputs": normal_values(part_keys[0], (LEN, 3, D), 1.0, 6.0, ((0, 4), (2, 4))),
        "short_filter": normal_values(key_of[1], (3, SHORT, D), SHORT ** -0.5, 3.5, ((2, 4),), jnp.float32),
        "medium_filter": normal_values(key_of[2], (MED, D), MED ** -0.5, 0.5, ((1, 4),), jnp.float32),
        "q_proj": draw_q_proj(jax.random.fold_in(jax.random.fold_in(key_of[6], part), 71), part),
        "k_proj": draw_k_proj(jax.random.fold_in(jax.random.fold_in(key_of[6], part), 71), part),
        "out_weight": normal_values(key_of[5], (D, D), (D // 16) ** -0.5, 0.25, ((0, 4),)),
    }


def shifted(array, shift_lag):
    widths = ((shift_lag, 0),) + ((0, 0),) * (array.ndim - 1)
    return jnp.pad(array, widths)[:array.shape[0]]


def reference(hyena_inputs, short_filter, medium_filter, q_proj, k_proj, out_weight):
    raw_inputs = hyena_inputs.astype(jnp.float32)
    filtered = jnp.zeros(raw_inputs.shape, jnp.float32)
    for shift_lag in range(SHORT):
        filtered = filtered + short_filter[:, shift_lag, :][None] * shifted(raw_inputs, shift_lag)
    product = (filtered[:, 1] * filtered[:, 2]).astype(jnp.bfloat16)
    product = lax.optimization_barrier(product).astype(jnp.float32)
    padded = jnp.pad(product, ((MED - 1, 0), (0, 0)))

    def add_tap(tap_index, summed):
        first_row = (MED - 1 - tap_index).astype(jnp.int32)
        zero_col = jnp.zeros((), jnp.int32)
        window = lax.dynamic_slice(padded, (first_row, zero_col), (LEN, D))
        return summed + medium_filter[tap_index][None] * window

    medium = lax.fori_loop(0, MED, add_tap, jnp.zeros((LEN, D), jnp.float32))
    hyena_out = (filtered[:, 0] * medium).astype(jnp.bfloat16)

    head_count = D // HEAD_SIZE
    score_scale = HEAD_SIZE ** -0.5
    query_heads = q_proj.reshape(LEN, head_count, HEAD_SIZE).transpose(1, 0, 2)
    key_heads = k_proj.reshape(LEN, head_count, HEAD_SIZE).transpose(1, 0, 2)
    value_heads = hyena_out.reshape(LEN, head_count, HEAD_SIZE).transpose(1, 0, 2)
    positions = jnp.arange(LEN, dtype=jnp.int32)
    allowed = positions[None, :] <= positions[:, None]

    def one_head(head_item):
        queries, keys, head_values = head_item
        scores = jnp.dot(queries, keys.T, preferred_element_type=jnp.float32) * score_scale
        masked = jnp.where(allowed, scores, -jnp.inf)
        row_top = jnp.max(masked, axis=-1, keepdims=True)
        weights = jnp.exp(masked - row_top)
        total_sum = jnp.sum(weights, axis=-1, keepdims=True)
        weighted = jnp.dot(weights.astype(jnp.bfloat16), head_values, preferred_element_type=jnp.float32)
        return (weighted / total_sum).astype(jnp.bfloat16)

    head_outputs = lax.map(one_head, (query_heads, key_heads, value_heads))
    attended = head_outputs.transpose(1, 0, 2).reshape(LEN, D)

    group_width = D // N_HEAD
    attended_groups = attended.reshape(LEN, N_HEAD, group_width).transpose(1, 0, 2)
    weight_groups = out_weight.reshape(N_HEAD, group_width, D)

    def add_group(summed, group_item):
        group_rows, group_weight = group_item
        partial_out = jnp.dot(group_rows, group_weight, preferred_element_type=jnp.float32).astype(jnp.bfloat16)
        partial_out = lax.optimization_barrier(partial_out).astype(jnp.float32)
        return summed + partial_out, None

    summed, unused = lax.scan(add_group, jnp.zeros((LEN, D), jnp.float32), (attended_groups, weight_groups))
    return (hyena_out, summed.astype(jnp.bfloat16))
```

```python
import functools

import jax
import jax.numpy as jnp
import numpy as np
from jax import lax
from jax.experimental import pallas as pl
from jax.experimental.pallas import tpu as pltpu
from jax.sharding import PartitionSpec as P

HEAD_SIZE = 128
MARGIN = 16
F32 = jnp.float32
BF16 = jnp.bfloat16


def passed_along(x, axis, by):
    length = lax.axis_size(axis)
    pairs = [(i, i + by) for i in range(length) if 0 <= i + by < length]
    return lax.ppermute(x, axis, pairs)


def high_low(x):
    high = x.astype(BF16)
    return high, (x - high.astype(F32)).astype(BF16)


def dot(a, b):
    return jnp.dot(a, b, preferred_element_type=F32)


def transform_tables(taps):
    size = 2 * taps
    freq = (2 * np.arange(taps)[:, None] + 1) * np.pi / size
    rows = np.arange(size)[None, :]
    forward = np.concatenate([np.cos(freq * rows), -np.sin(freq * rows)], 0)
    late = np.arange(taps, size)[:, None]
    inverse = np.concatenate([np.cos(freq.T * late), -np.sin(freq.T * late)], 1) * (2.0 / size)

    def split(table):
        high = table.astype(jnp.bfloat16)
        low = (table - high.astype(np.float64)).astype(jnp.bfloat16)
        return np.stack([high, low])

    return split(forward), split(inverse)


def short_filtered(ext, taps_ref, which):
    total = taps_ref[which, 0:1, :] * ext[MARGIN:]
    for lag in range(1, taps_ref.shape[1]):
        total += taps_ref[which, lag : lag + 1, :] * pltpu.roll(ext, lag, 0)[MARGIN:]
    return total


def tail_kernel(x_ref, short_ref, out_ref):
    parts = [short_filtered(x_ref[i].astype(F32), short_ref, i) for i in (1, 2)]
    out_ref[...] = (parts[0] * parts[1]).astype(BF16)


def filter_kernel(x_ref, halo_ref, tail_ref, short_ref, medium_ref, fwd_ref, inv_ref, out_ref):
    taps = medium_ref.shape[0]
    rows = x_ref.shape[1]
    filtered = []
    for i in range(3):
        ext = jnp.concatenate([halo_ref[i].astype(F32), x_ref[i].astype(F32)], 0)
        filtered.append(short_filtered(ext, short_ref, i))
    product = (filtered[1] * filtered[2]).astype(BF16)
    med_high, med_low = high_low(medium_ref[...])
    fwd_high, fwd_low = fwd_ref[0], fwd_ref[1]
    spectrum = (
        dot(fwd_high[:, :taps], med_high)
        + dot(fwd_high[:, :taps], med_low)
        + dot(fwd_low[:, :taps], med_high)
    )
    h_re, h_im = spectrum[:taps], spectrum[taps:]
    for b in range(rows // taps):
        before = tail_ref[...] if b == 0 else product[(b - 1) * taps : b * taps]
        window = jnp.concatenate([before, product[b * taps : (b + 1) * taps]], 0)
        x = dot(fwd_high, window) + dot(fwd_low, window)
        x_re, x_im = x[:taps], x[taps:]
        y = jnp.concatenate([x_re * h_re - x_im * h_im, x_re * h_im + x_im * h_re], 0)
        y_high, y_low = high_low(y)
        medium = dot(inv_ref[0], y_high) + dot(inv_ref[0], y_low) + dot(inv_ref[1], y_high)
        span = slice(b * taps, (b + 1) * taps)
        out_ref[span, :] = (filtered[0][span] * medium).astype(BF16)


def filter_block(hyena_inputs, short_filter, medium_filter):
    x = jnp.transpose(hyena_inputs, (1, 0, 2))
    _, rows, width = x.shape
    taps = medium_filter.shape[0]
    tile = min(256, width)
    halo = passed_along(x[:, rows - MARGIN :], "seq", 1)
    tail_rows = x[:, rows - taps - MARGIN :]
    by_col = lambda *lead: pl.BlockSpec((*lead, tile), lambda c: (0,) * len(lead) + (c,))
    whole = lambda a: pl.BlockSpec(a.shape, lambda c: (0,) * a.ndim)
    tail = pl.pallas_call(
        tail_kernel,
        grid=(width // tile,),
        out_shape=jax.ShapeDtypeStruct((taps, width), BF16),
        in_specs=[by_col(3, taps + MARGIN), by_col(3, short_filter.shape[1])],
        out_specs=by_col(taps),
    )(tail_rows, short_filter)
    tail = passed_along(tail, "seq", 1)
    forward, inverse = transform_tables(taps)
    return pl.pallas_call(
        filter_kernel,
        grid=(width // tile,),
        out_shape=jax.ShapeDtypeStruct((rows, width), BF16),
        in_specs=[
            by_col(3, rows),
            by_col(3, MARGIN),
            by_col(taps),
            by_col(3, short_filter.shape[1]),
            by_col(taps),
            whole(forward),
            whole(inverse),
        ],
        out_specs=by_col(rows),
        compiler_params=pltpu.CompilerParams(vmem_limit_bytes=56 * 2**20),
    )(x, halo, tail, short_filter, medium_filter, jnp.asarray(forward), jnp.asarray(inverse))


def attention_kernel(block, q_ref, k_ref, v_ref, out_ref, acc, top, total):
    rows = q_ref.shape[0]
    me = lax.axis_index("seq")
    scale = HEAD_SIZE ** (-0.5) * float(np.log2(np.e))
    acc[...] = jnp.zeros_like(acc)
    total[...] = jnp.zeros_like(total)
    top[...] = jnp.full_like(top, -1e30)

    def visit(start, diagonal):
        keys = k_ref[pl.ds(start, block), :]
        s = lax.dot_general(keys, q_ref[...], (((1,), (1,)), ((), ())), preferred_element_type=F32)
        if diagonal is not None:
            key_pos = lax.broadcasted_iota(jnp.int32, s.shape, 0) + diagonal
            query_pos = lax.broadcasted_iota(jnp.int32, s.shape, 1)
            s = jnp.where(key_pos <= query_pos, s, -1e30)
        new_top = jnp.maximum(top[...], jnp.max(s, axis=0, keepdims=True))
        weights = jnp.exp2(s * scale - new_top * scale)
        factor = jnp.exp2((top[...] - new_top) * scale)
        total[...] = total[...] * factor + jnp.sum(weights, axis=0, keepdims=True)
        acc[...] = acc[...] * factor + lax.dot_general(
            v_ref[pl.ds(start, block), :],
            weights.astype(BF16),
            (((0,), (0,)), ((), ())),
            preferred_element_type=F32,
        )
        top[...] = new_top

    def full(i, carry):
        visit(pl.multiple_of(i * block, block), None)
        return carry

    lax.fori_loop(0, me * (rows // block), full, 0)
    for j in range(rows // block):
        visit(pl.multiple_of(me * rows + j * block, block), j * block)
    out_ref[...] = (acc[...] / total[...]).T.astype(BF16)


def attention(q, keys, values):
    rows, width = q.shape
    one = lambda n: pl.BlockSpec((n, HEAD_SIZE), lambda h: (0, h))
    return pl.pallas_call(
        functools.partial(attention_kernel, rows),
        grid=(width // HEAD_SIZE,),
        out_shape=jax.ShapeDtypeStruct((rows, width), BF16),
        in_specs=[one(rows), one(keys.shape[0]), one(keys.shape[0])],
        out_specs=one(rows),
        scratch_shapes=[
            pltpu.VMEM((HEAD_SIZE, rows), F32),
            pltpu.VMEM((1, rows), F32),
            pltpu.VMEM((1, rows), F32),
        ],
        compiler_params=pltpu.CompilerParams(vmem_limit_bytes=56 * 2**20),
    )(q, keys, values)


def per_device(hyena_inputs, short_filter, medium_filter, q_proj, k_proj, out_weight):
    keys = lax.all_gather(k_proj, "seq", axis=0, tiled=True)
    hyena_out = filter_block(hyena_inputs, short_filter, medium_filter)
    values = lax.all_gather(hyena_out, "seq", axis=0, tiled=True)
    attended = attention(q_proj, keys, values)
    summed = lax.psum_scatter(
        lax.dot_general(
            out_weight, attended, (((0,), (1,)), ((), ())), preferred_element_type=F32
        ).astype(BF16),
        "head",
        scatter_dimension=0,
        tiled=True,
    )
    return (hyena_out, summed.T)


def solution(mesh):
    return jax.shard_map(
        per_device,
        mesh=mesh,
        in_specs=(
            P(("batch", "seq"), None, "head"),
            P(None, None, "head"),
            P(None, "head"),
            P(("batch", "seq"), "head"),
            P(("batch", "seq"), "head"),
            P("head", None),
        ),
        out_specs=(P(("batch", "seq"), "head"), P(("batch", "seq"), "head")),
        check_vma=False,
    )
```

```python
import functools
import math

import jax
import jax.numpy as jnp
import numpy as np
from jax import lax
from jax.experimental import pallas as pl
from jax.experimental.pallas import tpu as pltpu
from jax.sharding import PartitionSpec as P

HEAD_SIZE = 128
MARGIN = 16
F32 = jnp.float32
BF16 = jnp.bfloat16
MESH = pl.DeviceIdType.MESH


def passed_along(x, axis, by):
    length = lax.axis_size(axis)
    pairs = [(i, i + by) for i in range(length) if 0 <= i + by < length]
    return lax.ppermute(x, axis, pairs)


def high_low(x):
    high = x.astype(BF16)
    return high, (x - high.astype(F32)).astype(BF16)


def dot(a, b):
    return jnp.dot(a, b, preferred_element_type=F32)


def transform_tables(taps):
    size = 2 * taps
    freq = (2 * np.arange(taps)[:, None] + 1) * np.pi / size
    rows = np.arange(size)[None, :]
    forward = np.concatenate([np.cos(freq * rows), -np.sin(freq * rows)], 0)
    late = np.arange(taps, size)[:, None]
    inverse = np.concatenate([np.cos(freq.T * late), -np.sin(freq.T * late)], 1) * (2.0 / size)

    def split(table):
        high = table.astype(jnp.bfloat16)
        low = (table - high.astype(np.float64)).astype(jnp.bfloat16)
        return np.stack([high, low])

    return split(forward), split(inverse)


def short_filtered(ext, taps_ref, which):
    total = taps_ref[which, 0:1, :] * ext[MARGIN:]
    for lag in range(1, taps_ref.shape[1]):
        total += taps_ref[which, lag : lag + 1, :] * pltpu.roll(ext, lag, 0)[MARGIN:]
    return total


def tail_kernel(x_ref, short_ref, out_ref):
    parts = [short_filtered(x_ref[i].astype(F32), short_ref, i) for i in (1, 2)]
    out_ref[...] = (parts[0] * parts[1]).astype(BF16)


def filter_kernel(x_ref, halo_ref, tail_ref, short_ref, medium_ref, fwd_ref, inv_ref, out_ref):
    taps = medium_ref.shape[0]
    rows = x_ref.shape[1]
    filtered = []
    for i in range(3):
        ext = jnp.concatenate([halo_ref[i].astype(F32), x_ref[i].astype(F32)], 0)
        filtered.append(short_filtered(ext, short_ref, i))
    product = (filtered[1] * filtered[2]).astype(BF16)
    med_high, med_low = high_low(medium_ref[...])
    fwd_high, fwd_low = fwd_ref[0], fwd_ref[1]
    spectrum = (
        dot(fwd_high[:, :taps], med_high)
        + dot(fwd_high[:, :taps], med_low)
        + dot(fwd_low[:, :taps], med_high)
    )
    h_re, h_im = spectrum[:taps], spectrum[taps:]
    for b in range(rows // taps):
        before = tail_ref[...] if b == 0 else product[(b - 1) * taps : b * taps]
        window = jnp.concatenate([before, product[b * taps : (b + 1) * taps]], 0)
        x = dot(fwd_high, window) + dot(fwd_low, window)
        x_re, x_im = x[:taps], x[taps:]
        y = jnp.concatenate([x_re * h_re - x_im * h_im, x_re * h_im + x_im * h_re], 0)
        y_high, y_low = high_low(y)
        medium = dot(inv_ref[0], y_high) + dot(inv_ref[0], y_low) + dot(inv_ref[1], y_high)
        span = slice(b * taps, (b + 1) * taps)
        out_ref[span, :] = (filtered[0][span] * medium).astype(BF16)


def filter_block(hyena_inputs, short_filter, medium_filter):
    x = jnp.transpose(hyena_inputs, (1, 0, 2))
    _, rows, width = x.shape
    taps = medium_filter.shape[0]
    tile = min(256, width)
    halo = passed_along(x[:, rows - MARGIN :], "seq", 1)
    tail_rows = x[:, rows - taps - MARGIN :]
    by_col = lambda *lead: pl.BlockSpec((*lead, tile), lambda c: (0,) * len(lead) + (c,))
    whole = lambda a: pl.BlockSpec(a.shape, lambda c: (0,) * a.ndim)
    tail = pl.pallas_call(
        tail_kernel,
        grid=(width // tile,),
        out_shape=jax.ShapeDtypeStruct((taps, width), BF16),
        in_specs=[by_col(3, taps + MARGIN), by_col(3, short_filter.shape[1])],
        out_specs=by_col(taps),
    )(tail_rows, short_filter)
    tail = passed_along(tail, "seq", 1)
    forward, inverse = transform_tables(taps)
    return pl.pallas_call(
        filter_kernel,
        grid=(width // tile,),
        out_shape=jax.ShapeDtypeStruct((rows, width), BF16),
        in_specs=[
            by_col(3, rows),
            by_col(3, MARGIN),
            by_col(taps),
            by_col(3, short_filter.shape[1]),
            by_col(taps),
            whole(forward),
            whole(inverse),
        ],
        out_specs=by_col(rows),
        compiler_params=pltpu.CompilerParams(vmem_limit_bytes=56 * 2**20),
    )(x, halo, tail, short_filter, medium_filter, jnp.asarray(forward), jnp.asarray(inverse))


def attention_kernel(chips, groups, q_ref, *refs):
    pieces = 2 * chips
    key_refs, own_ref = refs[:pieces], refs[pieces]
    out_ref, got, acc, top, total, send_sem, recv_sem = refs[pieces + 1 :]
    rows = q_ref.shape[0]
    group_width = q_ref.shape[1] // groups
    me = lax.axis_index("seq")
    chip, core = lax.div(me, 2), lax.rem(me, 2)
    partner = me + 1 - 2 * core
    scale = HEAD_SIZE ** (-0.5) * float(np.log2(np.e))

    barrier = pltpu.get_barrier_semaphore()
    for step in range(1, chips):
        other = lax.rem(chip + step, chips) * 2 + core
        pl.semaphore_signal(barrier, inc=1, device_id={"seq": other}, device_id_type=MESH)
    pl.semaphore_signal(barrier, inc=1, device_id={"seq": partner}, device_id_type=MESH)
    pl.semaphore_wait(barrier, chips)

    def across(d, g):
        span = pl.ds(pl.multiple_of(g * group_width, HEAD_SIZE), group_width)
        return pltpu.make_async_remote_copy(
            src_ref=own_ref.at[:, span],
            dst_ref=got.at[d - 1, :, span],
            send_sem=send_sem.at[d - 1, g],
            recv_sem=recv_sem.at[d - 1, g],
            device_id={"seq": lax.rem(chip + d, chips) * 2 + core},
            device_id_type=MESH,
        )

    def beside(d, g):
        span = pl.ds(pl.multiple_of(g * group_width, HEAD_SIZE), group_width)
        source = own_ref.at[:, span] if d == 0 else got.at[d - 1, :, span]
        return pltpu.make_async_remote_copy(
            src_ref=source,
            dst_ref=got.at[chips - 1 + d, :, span],
            send_sem=send_sem.at[chips - 1 + d, g],
            recv_sem=recv_sem.at[chips - 1 + d, g],
            device_id={"seq": partner},
            device_id_type=MESH,
        )

    def send_group(g, carry):
        for d in range(1, chips):
            pl.when(chip + d < chips)(lambda d=d: across(d, g).start())
        pl.when(core == 0)(lambda: beside(0, g).start())
        return carry

    lax.fori_loop(0, groups, send_group, 0)

    def visit(keys, values, diagonal):
        s = lax.dot_general(keys[0], keys[1], (((1,), (1,)), ((), ())), preferred_element_type=F32)
        if diagonal:
            key_pos = lax.broadcasted_iota(jnp.int32, s.shape, 0)
            query_pos = lax.broadcasted_iota(jnp.int32, s.shape, 1)
            s = jnp.where(key_pos <= query_pos, s, -1e30)
        new_top = jnp.max(s, axis=0, keepdims=True)
        if not diagonal:
            new_top = jnp.maximum(top[...], new_top)
        weights = jnp.exp2(s * scale - new_top * scale)
        added = jnp.sum(weights, axis=0, keepdims=True)
        product = lax.dot_general(
            values, weights.astype(BF16), (((0,), (0,)), ((), ())), preferred_element_type=F32
        )
        if diagonal:
            total[...] = added
            acc[...] = product
        else:
            factor = jnp.exp2((top[...] - new_top) * scale)
            total[...] = total[...] * factor + added
            acc[...] = acc[...] * factor + product
        top[...] = new_top

    def one_group(g, carry):
        for d in range(1, chips):

            @pl.when(chip >= d)
            def _():
                across(d, g).wait_recv()
                beside(d, g).start()

        pl.when(core == 1)(lambda: beside(0, g).wait_recv())
        for d in range(1, chips):
            pl.when(chip >= d)(lambda d=d: beside(d, g).wait_recv())

        def one_head(h, carry):
            cols = pl.ds(pl.multiple_of(g * group_width + h * HEAD_SIZE, HEAD_SIZE), HEAD_SIZE)
            queries = q_ref[:, cols]
            visit((key_refs[0][:, cols], queries), own_ref[:, cols], True)

            @pl.when(core == 1)
            def _():
                visit((key_refs[chips][:, cols], queries), got[chips - 1, :, cols], False)

            for d in range(1, chips):

                @pl.when(chip >= d)
                def _():
                    visit((key_refs[d][:, cols], queries), got[d - 1, :, cols], False)
                    visit((key_refs[chips + d][:, cols], queries), got[chips - 1 + d, :, cols], False)

            out_ref[:, cols] = (acc[...] / total[...]).T.astype(BF16)
            return carry

        return lax.fori_loop(0, group_width // HEAD_SIZE, one_head, carry)

    lax.fori_loop(0, groups, one_group, 0)

    def finish(g, carry):
        for d in range(1, chips):
            pl.when(chip + d < chips)(lambda d=d: across(d, g).wait_send())
            pl.when(chip >= d)(lambda d=d: beside(d, g).wait_send())
        pl.when(core == 0)(lambda: beside(0, g).wait_send())
        return carry

    lax.fori_loop(0, groups, finish, 0)


def earlier_pieces(x):
    chips = lax.axis_size("seq") // 2
    mine, other = [x], []
    for d in range(1, chips):
        pairs = [(2 * i + k, 2 * (i + d) + k) for i in range(chips - d) for k in range(2)]
        mine.append(lax.ppermute(x, "seq", pairs))
    for d in range(chips):
        pairs = [(2 * i, 2 * i + 1) for i in range(d, chips)]
        if d > 0:
            pairs += [(2 * i + 1, 2 * i) for i in range(d, chips)]
        other.append(lax.ppermute(mine[d], "seq", pairs))
    return mine + other


def attention(q, key_pieces, values):
    rows, width = q.shape
    chips = len(key_pieces) // 2
    groups = math.gcd(width // HEAD_SIZE, 8)
    in_vmem = pl.BlockSpec(memory_space=pltpu.VMEM)
    return pl.pallas_call(
        functools.partial(attention_kernel, chips, groups),
        out_shape=jax.ShapeDtypeStruct((rows, width), BF16),
        in_specs=[in_vmem] * (2 * chips + 2),
        out_specs=in_vmem,
        scratch_shapes=[
            pltpu.VMEM((2 * chips - 1, rows, width), BF16),
            pltpu.VMEM((HEAD_SIZE, rows), F32),
            pltpu.VMEM((1, rows), F32),
            pltpu.VMEM((1, rows), F32),
            pltpu.SemaphoreType.DMA((2 * chips - 1, groups)),
            pltpu.SemaphoreType.DMA((2 * chips - 1, groups)),
        ],
        compiler_params=pltpu.CompilerParams(
            collective_id=1, has_side_effects=True, vmem_limit_bytes=56 * 2**20
        ),
    )(q, *key_pieces, values)


def project_kernel(n, chunk, att_ref, w_ref, out_ref, w_buf, slots, part, w_sem, send_sem, recv_sem):
    per_owner = out_ref.shape[1] // chunk
    me = lax.axis_index("head")
    up, down = n - 1 - me, me
    both = jnp.minimum(up, down)
    steps = n * per_owner

    def order(u):
        pair = lax.div(u, 2 * per_owner)
        within = lax.rem(u, 2 * per_owner)
        paired_owner = jnp.where(lax.rem(within, 2) == 0, n - 1 - pair, pair)
        single = both + lax.div(jnp.maximum(u - 2 * both * per_owner, 0), per_owner)
        single_owner = jnp.where(up > down, n - 1 - single, single)
        in_pairs = u < 2 * both * per_owner
        owner = jnp.where(in_pairs, paired_owner, single_owner)
        piece = jnp.where(in_pairs, lax.div(within, 2), lax.rem(u, per_owner))
        return jnp.where(u >= steps - per_owner, me, owner), piece

    def load(u):
        owner, piece = order(u)
        panel = owner * per_owner + piece
        columns = pl.ds(pl.multiple_of(panel * chunk, 128), chunk)
        return pltpu.make_async_copy(w_ref.at[:, columns], w_buf.at[panel], w_sem.at[panel]), panel

    def start_load(u, carry):
        load(u)[0].start()
        return carry

    lax.fori_loop(0, steps, start_load, 0)

    barrier = pltpu.get_barrier_semaphore()

    @pl.when(me > 0)
    def _():
        pl.semaphore_signal(barrier, inc=1, device_id={"head": me - 1}, device_id_type=MESH)

    @pl.when(me < n - 1)
    def _():
        pl.semaphore_signal(barrier, inc=1, device_id={"head": me + 1}, device_id_type=MESH)

    ends = (me == 0).astype(jnp.int32) + (me == n - 1).astype(jnp.int32)
    pl.semaphore_wait(barrier, 2 - ends)

    def passed(owner, piece):
        target = jnp.where(owner > me, me + 1, me - 1)
        slot = jnp.where(owner == me - 1, n, owner)
        return pltpu.make_async_remote_copy(
            src_ref=slots.at[owner, piece],
            dst_ref=slots.at[slot, piece],
            send_sem=send_sem.at[owner, piece],
            recv_sem=recv_sem.at[slot, piece],
            device_id={"head": target},
            device_id_type=MESH,
        )

    def arrived(slot, piece, source):
        return pltpu.make_async_remote_copy(
            src_ref=slots.at[slot, piece],
            dst_ref=slots.at[slot, piece],
            send_sem=send_sem.at[slot, piece],
            recv_sem=recv_sem.at[slot, piece],
            device_id={"head": source},
            device_id_type=MESH,
        )

    def one_step(u, carry):
        owner, piece = order(u)
        copy, panel = load(u)
        copy.wait()
        part[...] = dot(att_ref[...], w_buf[panel])

        @pl.when(u < steps - per_owner)
        def _():
            first = jnp.where(owner > me, me == 0, me == n - 1)

            @pl.when(first)
            def _():
                slots[owner, piece] = part[...].astype(BF16)

            @pl.when(jnp.logical_not(first))
            def _():
                arrived(owner, piece, jnp.where(owner > me, me - 1, me + 1)).wait_recv()
                slots[owner, piece] = (part[...] + slots[owner, piece].astype(F32)).astype(BF16)

            passed(owner, piece).start()

        @pl.when(u >= steps - per_owner)
        def _():
            @pl.when(me > 0)
            def _():
                arrived(me, piece, me - 1).wait_recv()
                part[...] += slots[me, piece].astype(F32)

            @pl.when(me < n - 1)
            def _():
                arrived(n, piece, me + 1).wait_recv()
                part[...] += slots[n, piece].astype(F32)

            columns = pl.ds(pl.multiple_of(piece * chunk, 128), chunk)
            out_ref[:, columns] = part[...].astype(BF16)

        return carry

    lax.fori_loop(0, steps, one_step, 0)

    def finish(u, carry):
        passed(*order(u)).wait_send()
        return carry

    lax.fori_loop(0, steps - per_owner, finish, 0)


def project(attended, out_weight):
    n = lax.axis_size("head")
    rows, depth = attended.shape
    columns = out_weight.shape[1] // n
    chunk = math.gcd(columns, 512)
    per_owner = columns // chunk
    in_vmem = pl.BlockSpec(memory_space=pltpu.VMEM)
    return pl.pallas_call(
        functools.partial(project_kernel, n, chunk),
        out_shape=jax.ShapeDtypeStruct((rows, columns), BF16),
        in_specs=[in_vmem, pl.BlockSpec(memory_space=pl.ANY)],
        out_specs=in_vmem,
        scratch_shapes=[
            pltpu.VMEM((n * per_owner, depth, chunk), BF16),
            pltpu.VMEM((n + 1, per_owner, rows, chunk), BF16),
            pltpu.VMEM((rows, chunk), F32),
            pltpu.SemaphoreType.DMA((n * per_owner,)),
            pltpu.SemaphoreType.DMA((n + 1, per_owner)),
            pltpu.SemaphoreType.DMA((n + 1, per_owner)),
        ],
        compiler_params=pltpu.CompilerParams(
            collective_id=2, has_side_effects=True, vmem_limit_bytes=60 * 2**20
        ),
    )(attended, out_weight)


def per_device(hyena_inputs, short_filter, medium_filter, q_proj, k_proj, out_weight):
    key_pieces = earlier_pieces(k_proj)
    hyena_out = filter_block(hyena_inputs, short_filter, medium_filter)
    attended = attention(q_proj, key_pieces, hyena_out)
    return (hyena_out, project(attended, out_weight))


def solution(mesh):
    return jax.shard_map(
        per_device,
        mesh=mesh,
        in_specs=(
            P(("batch", "seq"), None, "head"),
            P(None, None, "head"),
            P(None, "head"),
            P(("batch", "seq"), "head"),
            P(("batch", "seq"), "head"),
            P("head", None),
        ),
        out_specs=(P(("batch", "seq"), "head"), P(("batch", "seq"), "head")),
        check_vma=False,
    )
```

```python
import functools
import math

import jax
import jax.numpy as jnp
import numpy as np
from jax import lax
from jax.experimental import pallas as pl
from jax.experimental.pallas import tpu as pltpu
from jax.sharding import PartitionSpec as P

HEAD_SIZE = 128
MARGIN = 16
F32 = jnp.float32
BF16 = jnp.bfloat16
MESH = pl.DeviceIdType.MESH


def passed_along(x, axis, by):
    length = lax.axis_size(axis)
    pairs = [(i, i + by) for i in range(length) if 0 <= i + by < length]
    return lax.ppermute(x, axis, pairs)


def high_low(x):
    high = x.astype(BF16)
    return high, (x - high.astype(F32)).astype(BF16)


def dot(a, b):
    return jnp.dot(a, b, preferred_element_type=F32)


def transform_tables(taps):
    size = 2 * taps
    freq = (2 * np.arange(taps)[:, None] + 1) * np.pi / size
    rows = np.arange(size)[None, :]
    forward = np.concatenate([np.cos(freq * rows), -np.sin(freq * rows)], 0)
    late = np.arange(taps, size)[:, None]
    inverse = np.concatenate([np.cos(freq.T * late), -np.sin(freq.T * late)], 1) * (2.0 / size)

    def split(table):
        high = table.astype(jnp.bfloat16)
        low = (table - high.astype(np.float64)).astype(jnp.bfloat16)
        return np.stack([high, low])

    return split(forward), split(inverse)


def short_filtered(ext, taps_ref, which):
    total = taps_ref[which, 0:1, :] * ext[MARGIN:]
    for lag in range(1, taps_ref.shape[1]):
        total += taps_ref[which, lag : lag + 1, :] * pltpu.roll(ext, lag, 0)[MARGIN:]
    return total


def tail_kernel(x_ref, short_ref, out_ref):
    start = x_ref.shape[1] - out_ref.shape[0] - MARGIN
    parts = [short_filtered(x_ref[i, start:].astype(F32), short_ref, i) for i in (1, 2)]
    out_ref[...] = (parts[0] * parts[1]).astype(BF16)


def filter_kernel(x_ref, halo_ref, tail_ref, short_ref, medium_ref, fwd_ref, inv_ref, out_ref):
    taps = medium_ref.shape[0]
    rows = x_ref.shape[1]
    filtered = []
    for i in range(3):
        ext = jnp.concatenate([halo_ref[i].astype(F32), x_ref[i].astype(F32)], 0)
        filtered.append(short_filtered(ext, short_ref, i))
    product = (filtered[1] * filtered[2]).astype(BF16)
    med_high, med_low = high_low(medium_ref[...])
    fwd_high, fwd_low = fwd_ref[0], fwd_ref[1]
    spectrum = (
        dot(fwd_high[:, :taps], med_high)
        + dot(fwd_high[:, :taps], med_low)
        + dot(fwd_low[:, :taps], med_high)
    )
    h_re, h_im = spectrum[:taps], spectrum[taps:]
    for b in range(rows // taps):
        before = tail_ref[...] if b == 0 else product[(b - 1) * taps : b * taps]
        window = jnp.concatenate([before, product[b * taps : (b + 1) * taps]], 0)
        x = dot(fwd_high, window) + dot(fwd_low, window)
        x_re, x_im = x[:taps], x[taps:]
        y = jnp.concatenate([x_re * h_re - x_im * h_im, x_re * h_im + x_im * h_re], 0)
        y_high, y_low = high_low(y)
        medium = dot(inv_ref[0], y_high) + dot(inv_ref[0], y_low) + dot(inv_ref[1], y_high)
        span = slice(b * taps, (b + 1) * taps)
        out_ref[span, :] = (filtered[0][span] * medium).astype(BF16)


def filter_block(hyena_inputs, short_filter, medium_filter):
    x = jnp.transpose(hyena_inputs, (1, 0, 2))
    _, rows, width = x.shape
    taps = medium_filter.shape[0]
    tile = min(256, width)
    halo = passed_along(x[:, rows - MARGIN :], "seq", 1)
    by_col = lambda *lead: pl.BlockSpec((*lead, tile), lambda c: (0,) * len(lead) + (c,))
    whole = lambda a: pl.BlockSpec(a.shape, lambda c: (0,) * a.ndim)
    tail = pl.pallas_call(
        tail_kernel,
        grid=(width // tile,),
        out_shape=jax.ShapeDtypeStruct((taps, width), BF16),
        in_specs=[
            pl.BlockSpec((3, rows // 2, tile), lambda c: (0, 1, c)),
            by_col(3, short_filter.shape[1]),
        ],
        out_specs=by_col(taps),
    )(x, short_filter)
    tail = passed_along(tail, "seq", 1)
    forward, inverse = transform_tables(taps)
    return pl.pallas_call(
        filter_kernel,
        grid=(width // tile,),
        out_shape=jax.ShapeDtypeStruct((rows, width), BF16),
        in_specs=[
            by_col(3, rows),
            by_col(3, MARGIN),
            by_col(taps),
            by_col(3, short_filter.shape[1]),
            by_col(taps),
            whole(forward),
            whole(inverse),
        ],
        out_specs=by_col(rows),
        compiler_params=pltpu.CompilerParams(vmem_limit_bytes=56 * 2**20),
    )(x, halo, tail, short_filter, medium_filter, jnp.asarray(forward), jnp.asarray(inverse))


def attention_kernel(chips, groups, q_ref, *refs):
    key_refs, own_ref = refs[:chips], refs[chips]
    (
        out_ref, got, got_keys, acc, top, total,
        send_sem, recv_sem, key_send_sem, key_recv_sem,
    ) = refs[chips + 1 :]
    rows = q_ref.shape[0]
    group_width = q_ref.shape[1] // groups
    me = lax.axis_index("seq")
    chip, core = lax.div(me, 2), lax.rem(me, 2)
    partner = me + 1 - 2 * core
    scale = HEAD_SIZE ** (-0.5) * float(np.log2(np.e))

    barrier = pltpu.get_barrier_semaphore()
    for step in range(1, chips):
        other = lax.rem(chip + step, chips) * 2 + core
        pl.semaphore_signal(barrier, inc=1, device_id={"seq": other}, device_id_type=MESH)
    pl.semaphore_signal(barrier, inc=1, device_id={"seq": partner}, device_id_type=MESH)
    pl.semaphore_wait(barrier, chips)

    def across(d, g):
        span = pl.ds(pl.multiple_of(g * group_width, HEAD_SIZE), group_width)
        return pltpu.make_async_remote_copy(
            src_ref=own_ref.at[:, span],
            dst_ref=got.at[d - 1, :, span],
            send_sem=send_sem.at[d - 1, g],
            recv_sem=recv_sem.at[d - 1, g],
            device_id={"seq": lax.rem(chip + d, chips) * 2 + core},
            device_id_type=MESH,
        )

    def beside(d, g):
        span = pl.ds(pl.multiple_of(g * group_width, HEAD_SIZE), group_width)
        source = own_ref.at[:, span] if d == 0 else got.at[d - 1, :, span]
        return pltpu.make_async_remote_copy(
            src_ref=source,
            dst_ref=got.at[chips - 1 + d, :, span],
            send_sem=send_sem.at[chips - 1 + d, g],
            recv_sem=recv_sem.at[chips - 1 + d, g],
            device_id={"seq": partner},
            device_id_type=MESH,
        )

    def beside_keys(d, g):
        span = pl.ds(pl.multiple_of(g * group_width, HEAD_SIZE), group_width)
        return pltpu.make_async_remote_copy(
            src_ref=key_refs[d].at[:, span],
            dst_ref=got_keys.at[d, :, span],
            send_sem=key_send_sem.at[d, g],
            recv_sem=key_recv_sem.at[d, g],
            device_id={"seq": partner},
            device_id_type=MESH,
        )

    def send_group(g, carry):
        for d in range(1, chips):
            pl.when(chip + d < chips)(lambda d=d: across(d, g).start())
        pl.when(core == 0)(lambda: beside_keys(0, g).start())
        pl.when(core == 0)(lambda: beside(0, g).start())
        for d in range(1, chips):
            pl.when(chip >= d)(lambda d=d: beside_keys(d, g).start())
        return carry

    lax.fori_loop(0, groups, send_group, 0)

    def visit(keys, values, diagonal):
        s = lax.dot_general(keys[0], keys[1], (((1,), (1,)), ((), ())), preferred_element_type=F32)
        if diagonal:
            key_pos = lax.broadcasted_iota(jnp.int32, s.shape, 0)
            query_pos = lax.broadcasted_iota(jnp.int32, s.shape, 1)
            s = jnp.where(key_pos <= query_pos, s, -1e30)
        new_top = jnp.max(s, axis=0, keepdims=True)
        if not diagonal:
            new_top = jnp.maximum(top[...], new_top)
        weights = jnp.exp2(s * scale - new_top * scale)
        added = jnp.sum(weights, axis=0, keepdims=True)
        product = lax.dot_general(
            values, weights.astype(BF16), (((0,), (0,)), ((), ())), preferred_element_type=F32
        )
        if diagonal:
            total[...] = added
            acc[...] = product
        else:
            factor = jnp.exp2((top[...] - new_top) * scale)
            total[...] = total[...] * factor + added
            acc[...] = acc[...] * factor + product
        top[...] = new_top

    def one_group(g, carry):
        for d in range(1, chips):

            @pl.when(chip >= d)
            def _():
                across(d, g).wait_recv()
                beside(d, g).start()

        @pl.when(core == 1)
        def _():
            beside_keys(0, g).wait_recv()
            beside(0, g).wait_recv()

        for d in range(1, chips):

            @pl.when(chip >= d)
            def _():
                beside_keys(d, g).wait_recv()
                beside(d, g).wait_recv()

        def one_head(h, carry):
            cols = pl.ds(pl.multiple_of(g * group_width + h * HEAD_SIZE, HEAD_SIZE), HEAD_SIZE)
            queries = q_ref[:, cols]
            visit((key_refs[0][:, cols], queries), own_ref[:, cols], True)

            @pl.when(core == 1)
            def _():
                visit((got_keys[0, :, cols], queries), got[chips - 1, :, cols], False)

            for d in range(1, chips):

                @pl.when(chip >= d)
                def _():
                    visit((key_refs[d][:, cols], queries), got[d - 1, :, cols], False)
                    visit((got_keys[d, :, cols], queries), got[chips - 1 + d, :, cols], False)

            out_ref[:, cols] = (acc[...] / total[...]).T.astype(BF16)
            return carry

        return lax.fori_loop(0, group_width // HEAD_SIZE, one_head, carry)

    lax.fori_loop(0, groups, one_group, 0)

    def finish(g, carry):
        for d in range(1, chips):
            pl.when(chip + d < chips)(lambda d=d: across(d, g).wait_send())
            pl.when(chip >= d)(lambda d=d: beside(d, g).wait_send())
            pl.when(chip >= d)(lambda d=d: beside_keys(d, g).wait_send())
        pl.when(core == 0)(lambda: beside(0, g).wait_send())
        pl.when(core == 0)(lambda: beside_keys(0, g).wait_send())
        return carry

    lax.fori_loop(0, groups, finish, 0)


def earlier_pieces(x):
    chips = lax.axis_size("seq") // 2
    mine = [x]
    for d in range(1, chips):
        pairs = [(2 * i + k, 2 * (i + d) + k) for i in range(chips - d) for k in range(2)]
        mine.append(lax.ppermute(x, "seq", pairs))
    return mine


def attention(q, key_pieces, values):
    rows, width = q.shape
    chips = len(key_pieces)
    groups = math.gcd(width // HEAD_SIZE, 8)
    in_vmem = pl.BlockSpec(memory_space=pltpu.VMEM)
    return pl.pallas_call(
        functools.partial(attention_kernel, chips, groups),
        out_shape=jax.ShapeDtypeStruct((rows, width), BF16),
        in_specs=[in_vmem] * (chips + 2),
        out_specs=in_vmem,
        scratch_shapes=[
            pltpu.VMEM((2 * chips - 1, rows, width), BF16),
            pltpu.VMEM((chips, rows, width), BF16),
            pltpu.VMEM((HEAD_SIZE, rows), F32),
            pltpu.VMEM((1, rows), F32),
            pltpu.VMEM((1, rows), F32),
            pltpu.SemaphoreType.DMA((2 * chips - 1, groups)),
            pltpu.SemaphoreType.DMA((2 * chips - 1, groups)),
            pltpu.SemaphoreType.DMA((chips, groups)),
            pltpu.SemaphoreType.DMA((chips, groups)),
        ],
        compiler_params=pltpu.CompilerParams(
            collective_id=1, has_side_effects=True, vmem_limit_bytes=56 * 2**20
        ),
    )(q, *key_pieces, values)


def project_kernel(n, chunk, att_ref, w_ref, out_ref, w_buf, slots, part, w_sem, send_sem, recv_sem):
    per_owner = out_ref.shape[1] // chunk
    me = lax.axis_index("head")
    up, down = n - 1 - me, me
    both = jnp.minimum(up, down)
    steps = n * per_owner

    def order(u):
        pair = lax.div(u, 2 * per_owner)
        within = lax.rem(u, 2 * per_owner)
        paired_owner = jnp.where(lax.rem(within, 2) == 0, n - 1 - pair, pair)
        single = both + lax.div(jnp.maximum(u - 2 * both * per_owner, 0), per_owner)
        single_owner = jnp.where(up > down, n - 1 - single, single)
        in_pairs = u < 2 * both * per_owner
        owner = jnp.where(in_pairs, paired_owner, single_owner)
        piece = jnp.where(in_pairs, lax.div(within, 2), lax.rem(u, per_owner))
        return jnp.where(u >= steps - per_owner, me, owner), piece

    def load(u):
        owner, piece = order(u)
        panel = owner * per_owner + piece
        columns = pl.ds(pl.multiple_of(panel * chunk, 128), chunk)
        return pltpu.make_async_copy(w_ref.at[:, columns], w_buf.at[panel], w_sem.at[panel]), panel

    def start_load(u, carry):
        load(u)[0].start()
        return carry

    lax.fori_loop(0, steps, start_load, 0)

    barrier = pltpu.get_barrier_semaphore()

    @pl.when(me > 0)
    def _():
        pl.semaphore_signal(barrier, inc=1, device_id={"head": me - 1}, device_id_type=MESH)

    @pl.when(me < n - 1)
    def _():
        pl.semaphore_signal(barrier, inc=1, device_id={"head": me + 1}, device_id_type=MESH)

    ends = (me == 0).astype(jnp.int32) + (me == n - 1).astype(jnp.int32)
    pl.semaphore_wait(barrier, 2 - ends)

    def passed(owner, piece):
        target = jnp.where(owner > me, me + 1, me - 1)
        slot = jnp.where(owner == me - 1, n, owner)
        return pltpu.make_async_remote_copy(
            src_ref=slots.at[owner, piece],
            dst_ref=slots.at[slot, piece],
            send_sem=send_sem.at[owner, piece],
            recv_sem=recv_sem.at[slot, piece],
            device_id={"head": target},
            device_id_type=MESH,
        )

    def arrived(slot, piece, source):
        return pltpu.make_async_remote_copy(
            src_ref=slots.at[slot, piece],
            dst_ref=slots.at[slot, piece],
            send_sem=send_sem.at[slot, piece],
            recv_sem=recv_sem.at[slot, piece],
            device_id={"head": source},
            device_id_type=MESH,
        )

    def one_step(u, carry):
        owner, piece = order(u)
        copy, panel = load(u)
        copy.wait()
        part[...] = dot(att_ref[...], w_buf[panel])

        @pl.when(u < steps - per_owner)
        def _():
            first = jnp.where(owner > me, me == 0, me == n - 1)

            @pl.when(first)
            def _():
                slots[owner, piece] = part[...].astype(BF16)

            @pl.when(jnp.logical_not(first))
            def _():
                arrived(owner, piece, jnp.where(owner > me, me - 1, me + 1)).wait_recv()
                slots[owner, piece] = (part[...] + slots[owner, piece].astype(F32)).astype(BF16)

            passed(owner, piece).start()

        @pl.when(u >= steps - per_owner)
        def _():
            @pl.when(me > 0)
            def _():
                arrived(me, piece, me - 1).wait_recv()
                part[...] += slots[me, piece].astype(F32)

            @pl.when(me < n - 1)
            def _():
                arrived(n, piece, me + 1).wait_recv()
                part[...] += slots[n, piece].astype(F32)

            columns = pl.ds(pl.multiple_of(piece * chunk, 128), chunk)
            out_ref[:, columns] = part[...].astype(BF16)

        return carry

    lax.fori_loop(0, steps, one_step, 0)

    def finish(u, carry):
        passed(*order(u)).wait_send()
        return carry

    lax.fori_loop(0, steps - per_owner, finish, 0)


def project(attended, out_weight):
    n = lax.axis_size("head")
    rows, depth = attended.shape
    columns = out_weight.shape[1] // n
    chunk = math.gcd(columns, 512)
    per_owner = columns // chunk
    in_vmem = pl.BlockSpec(memory_space=pltpu.VMEM)
    return pl.pallas_call(
        functools.partial(project_kernel, n, chunk),
        out_shape=jax.ShapeDtypeStruct((rows, columns), BF16),
        in_specs=[in_vmem, pl.BlockSpec(memory_space=pl.ANY)],
        out_specs=in_vmem,
        scratch_shapes=[
            pltpu.VMEM((n * per_owner, depth, chunk), BF16),
            pltpu.VMEM((n + 1, per_owner, rows, chunk), BF16),
            pltpu.VMEM((rows, chunk), F32),
            pltpu.SemaphoreType.DMA((n * per_owner,)),
            pltpu.SemaphoreType.DMA((n + 1, per_owner)),
            pltpu.SemaphoreType.DMA((n + 1, per_owner)),
        ],
        compiler_params=pltpu.CompilerParams(
            collective_id=2, has_side_effects=True, vmem_limit_bytes=60 * 2**20
        ),
    )(attended, out_weight)


def per_device(hyena_inputs, short_filter, medium_filter, q_proj, k_proj, out_weight):
    key_pieces = earlier_pieces(k_proj)
    hyena_out = filter_block(hyena_inputs, short_filter, medium_filter)
    attended = attention(q_proj, key_pieces, hyena_out)
    return (hyena_out, project(attended, out_weight))


def solution(mesh):
    return jax.shard_map(
        per_device,
        mesh=mesh,
        in_specs=(
            P(("batch", "seq"), None, "head"),
            P(None, None, "head"),
            P(None, "head"),
            P(("batch", "seq"), "head"),
            P(("batch", "seq"), "head"),
            P("head", None),
        ),
        out_specs=(P(("batch", "seq"), "head"), P(("batch", "seq"), "head")),
        check_vma=False,
    )
```

```python
import functools
import math

import jax
import jax.numpy as jnp
import numpy as np
from jax import lax
from jax.experimental import pallas as pl
from jax.experimental.pallas import tpu as pltpu
from jax.sharding import PartitionSpec as P

HEAD_SIZE = 128
MARGIN = 16
F32 = jnp.float32
BF16 = jnp.bfloat16
MESH = pl.DeviceIdType.MESH


def passed_along(x, axis, by):
    length = lax.axis_size(axis)
    pairs = [(i, i + by) for i in range(length) if 0 <= i + by < length]
    return lax.ppermute(x, axis, pairs)


def high_low(x):
    high = x.astype(BF16)
    return high, (x - high.astype(F32)).astype(BF16)


def dot(a, b):
    return jnp.dot(a, b, preferred_element_type=F32)


def transform_tables(taps):
    size = 2 * taps
    freq = (2 * np.arange(taps)[:, None] + 1) * np.pi / size
    rows = np.arange(size)[None, :]
    forward = np.concatenate([np.cos(freq * rows), -np.sin(freq * rows)], 0)
    late = np.arange(taps, size)[:, None]
    inverse = np.concatenate([np.cos(freq.T * late), -np.sin(freq.T * late)], 1) * (2.0 / size)

    def split(table):
        high = table.astype(jnp.bfloat16)
        low = (table - high.astype(np.float64)).astype(jnp.bfloat16)
        return np.stack([high, low])

    return split(forward), split(inverse)


def short_filtered(ext, taps_ref, which):
    total = taps_ref[which, 0:1, :] * ext[MARGIN:]
    for lag in range(1, taps_ref.shape[1]):
        total += taps_ref[which, lag : lag + 1, :] * pltpu.roll(ext, lag, 0)[MARGIN:]
    return total


def tail_kernel(x_ref, short_ref, out_ref):
    start = x_ref.shape[1] - out_ref.shape[0] - MARGIN
    parts = [short_filtered(x_ref[i, start:].astype(F32), short_ref, i) for i in (1, 2)]
    out_ref[...] = (parts[0] * parts[1]).astype(BF16)


def filter_kernel(x_ref, halo_ref, tail_ref, short_ref, medium_ref, fwd_ref, inv_ref, out_ref):
    taps = medium_ref.shape[0]
    rows = x_ref.shape[1]
    filtered = []
    for i in range(3):
        ext = jnp.concatenate([halo_ref[i].astype(F32), x_ref[i].astype(F32)], 0)
        filtered.append(short_filtered(ext, short_ref, i))
    product = (filtered[1] * filtered[2]).astype(BF16)
    med_high, med_low = high_low(medium_ref[...])
    fwd_high, fwd_low = fwd_ref[0], fwd_ref[1]
    spectrum = (
        dot(fwd_high[:, :taps], med_high)
        + dot(fwd_high[:, :taps], med_low)
        + dot(fwd_low[:, :taps], med_high)
    )
    h_re, h_im = spectrum[:taps], spectrum[taps:]
    for b in range(rows // taps):
        before = tail_ref[...] if b == 0 else product[(b - 1) * taps : b * taps]
        window = jnp.concatenate([before, product[b * taps : (b + 1) * taps]], 0)
        x = dot(fwd_high, window) + dot(fwd_low, window)
        x_re, x_im = x[:taps], x[taps:]
        y = jnp.concatenate([x_re * h_re - x_im * h_im, x_re * h_im + x_im * h_re], 0)
        y_high, y_low = high_low(y)
        medium = dot(inv_ref[0], y_high) + dot(inv_ref[0], y_low) + dot(inv_ref[1], y_high)
        span = slice(b * taps, (b + 1) * taps)
        out_ref[span, :] = (filtered[0][span] * medium).astype(BF16)


def filter_block(hyena_inputs, short_filter, medium_filter, k_proj):
    x = jnp.transpose(hyena_inputs, (1, 0, 2))
    _, rows, width = x.shape
    taps = medium_filter.shape[0]
    tile = min(256, width)
    halo = passed_along(x[:, rows - MARGIN :], "seq", 1)
    by_col = lambda *lead: pl.BlockSpec((*lead, tile), lambda c: (0,) * len(lead) + (c,))
    whole = lambda a: pl.BlockSpec(a.shape, lambda c: (0,) * a.ndim)
    tail = pl.pallas_call(
        tail_kernel,
        grid=(width // tile,),
        out_shape=jax.ShapeDtypeStruct((taps, width), BF16),
        in_specs=[
            pl.BlockSpec((3, rows // 2, tile), lambda c: (0, 1, c)),
            by_col(3, short_filter.shape[1]),
        ],
        out_specs=by_col(taps),
    )(x, short_filter)
    tail = passed_along(tail, "seq", 1)
    tail, halo, k_proj = lax.optimization_barrier((tail, halo, k_proj))
    key_pieces = earlier_pieces(k_proj)
    forward, inverse = transform_tables(taps)
    hyena_out = pl.pallas_call(
        filter_kernel,
        grid=(width // tile,),
        out_shape=jax.ShapeDtypeStruct((rows, width), BF16),
        in_specs=[
            by_col(3, rows),
            by_col(3, MARGIN),
            by_col(taps),
            by_col(3, short_filter.shape[1]),
            by_col(taps),
            whole(forward),
            whole(inverse),
        ],
        out_specs=by_col(rows),
        compiler_params=pltpu.CompilerParams(vmem_limit_bytes=56 * 2**20),
    )(x, halo, tail, short_filter, medium_filter, jnp.asarray(forward), jnp.asarray(inverse))
    return hyena_out, key_pieces


def attention_kernel(chips, groups, q_ref, *refs):
    key_refs, own_ref = refs[:chips], refs[chips]
    (
        out_ref, got, got_keys, acc, top, total,
        send_sem, recv_sem, key_send_sem, key_recv_sem,
    ) = refs[chips + 1 :]
    rows = q_ref.shape[0]
    group_width = q_ref.shape[1] // groups
    me = lax.axis_index("seq")
    chip, core = lax.div(me, 2), lax.rem(me, 2)
    partner = me + 1 - 2 * core
    scale = HEAD_SIZE ** (-0.5) * float(np.log2(np.e))

    barrier = pltpu.get_barrier_semaphore()
    for step in range(1, chips):
        other = lax.rem(chip + step, chips) * 2 + core
        pl.semaphore_signal(barrier, inc=1, device_id={"seq": other}, device_id_type=MESH)
    pl.semaphore_signal(barrier, inc=1, device_id={"seq": partner}, device_id_type=MESH)
    pl.semaphore_wait(barrier, chips)

    def across(d, g):
        span = pl.ds(pl.multiple_of(g * group_width, HEAD_SIZE), group_width)
        return pltpu.make_async_remote_copy(
            src_ref=own_ref.at[:, span],
            dst_ref=got.at[d - 1, :, span],
            send_sem=send_sem.at[d - 1, g],
            recv_sem=recv_sem.at[d - 1, g],
            device_id={"seq": lax.rem(chip + d, chips) * 2 + core},
            device_id_type=MESH,
        )

    def beside(d, g):
        span = pl.ds(pl.multiple_of(g * group_width, HEAD_SIZE), group_width)
        source = own_ref.at[:, span] if d == 0 else got.at[d - 1, :, span]
        return pltpu.make_async_remote_copy(
            src_ref=source,
            dst_ref=got.at[chips - 1 + d, :, span],
            send_sem=send_sem.at[chips - 1 + d, g],
            recv_sem=recv_sem.at[chips - 1 + d, g],
            device_id={"seq": partner},
            device_id_type=MESH,
        )

    def beside_keys(d, g):
        span = pl.ds(pl.multiple_of(g * group_width, HEAD_SIZE), group_width)
        return pltpu.make_async_remote_copy(
            src_ref=key_refs[d].at[:, span],
            dst_ref=got_keys.at[d, :, span],
            send_sem=key_send_sem.at[d, g],
            recv_sem=key_recv_sem.at[d, g],
            device_id={"seq": partner},
            device_id_type=MESH,
        )

    def send_group(g, carry):
        for d in range(1, chips):
            pl.when(chip + d < chips)(lambda d=d: across(d, g).start())
        pl.when(core == 0)(lambda: beside_keys(0, g).start())
        pl.when(core == 0)(lambda: beside(0, g).start())
        for d in range(1, chips):
            pl.when(chip >= d)(lambda d=d: beside_keys(d, g).start())
        return carry

    lax.fori_loop(0, groups, send_group, 0)

    def visit(keys, values, diagonal):
        s = lax.dot_general(keys[0], keys[1], (((1,), (1,)), ((), ())), preferred_element_type=F32)
        if diagonal:
            key_pos = lax.broadcasted_iota(jnp.int32, s.shape, 0)
            query_pos = lax.broadcasted_iota(jnp.int32, s.shape, 1)
            s = jnp.where(key_pos <= query_pos, s, -1e30)
        new_top = jnp.max(s, axis=0, keepdims=True)
        if not diagonal:
            new_top = jnp.maximum(top[...], new_top)
        weights = jnp.exp2(s * scale - new_top * scale)
        added = jnp.sum(weights, axis=0, keepdims=True)
        product = lax.dot_general(
            values, weights.astype(BF16), (((0,), (0,)), ((), ())), preferred_element_type=F32
        )
        if diagonal:
            total[...] = added
            acc[...] = product
        else:
            factor = jnp.exp2((top[...] - new_top) * scale)
            total[...] = total[...] * factor + added
            acc[...] = acc[...] * factor + product
        top[...] = new_top

    def one_group(g, carry):
        for d in range(1, chips):

            @pl.when(chip >= d)
            def _():
                across(d, g).wait_recv()
                beside(d, g).start()

        @pl.when(core == 1)
        def _():
            beside_keys(0, g).wait_recv()
            beside(0, g).wait_recv()

        for d in range(1, chips):

            @pl.when(chip >= d)
            def _():
                beside_keys(d, g).wait_recv()
                beside(d, g).wait_recv()

        def one_head(h, carry):
            cols = pl.ds(pl.multiple_of(g * group_width + h * HEAD_SIZE, HEAD_SIZE), HEAD_SIZE)
            queries = q_ref[:, cols]
            visit((key_refs[0][:, cols], queries), own_ref[:, cols], True)

            @pl.when(core == 1)
            def _():
                visit((got_keys[0, :, cols], queries), got[chips - 1, :, cols], False)

            for d in range(1, chips):

                @pl.when(chip >= d)
                def _():
                    visit((key_refs[d][:, cols], queries), got[d - 1, :, cols], False)
                    visit((got_keys[d, :, cols], queries), got[chips - 1 + d, :, cols], False)

            out_ref[:, cols] = (acc[...] / total[...]).T.astype(BF16)
            return carry

        return lax.fori_loop(0, group_width // HEAD_SIZE, one_head, carry)

    lax.fori_loop(0, groups, one_group, 0)

    def finish(g, carry):
        for d in range(1, chips):
            pl.when(chip + d < chips)(lambda d=d: across(d, g).wait_send())
            pl.when(chip >= d)(lambda d=d: beside(d, g).wait_send())
            pl.when(chip >= d)(lambda d=d: beside_keys(d, g).wait_send())
        pl.when(core == 0)(lambda: beside(0, g).wait_send())
        pl.when(core == 0)(lambda: beside_keys(0, g).wait_send())
        return carry

    lax.fori_loop(0, groups, finish, 0)


def earlier_pieces(x):
    chips = lax.axis_size("seq") // 2
    mine = [x]
    for d in range(1, chips):
        pairs = [(2 * i + k, 2 * (i + d) + k) for i in range(chips - d) for k in range(2)]
        mine.append(lax.ppermute(x, "seq", pairs))
    return mine


def attention(q, key_pieces, values):
    rows, width = q.shape
    chips = len(key_pieces)
    groups = math.gcd(width // HEAD_SIZE, 8)
    in_vmem = pl.BlockSpec(memory_space=pltpu.VMEM)
    return pl.pallas_call(
        functools.partial(attention_kernel, chips, groups),
        out_shape=jax.ShapeDtypeStruct((rows, width), BF16),
        in_specs=[in_vmem] * (chips + 2),
        out_specs=in_vmem,
        scratch_shapes=[
            pltpu.VMEM((2 * chips - 1, rows, width), BF16),
            pltpu.VMEM((chips, rows, width), BF16),
            pltpu.VMEM((HEAD_SIZE, rows), F32),
            pltpu.VMEM((1, rows), F32),
            pltpu.VMEM((1, rows), F32),
            pltpu.SemaphoreType.DMA((2 * chips - 1, groups)),
            pltpu.SemaphoreType.DMA((2 * chips - 1, groups)),
            pltpu.SemaphoreType.DMA((chips, groups)),
            pltpu.SemaphoreType.DMA((chips, groups)),
        ],
        compiler_params=pltpu.CompilerParams(
            collective_id=1, has_side_effects=True, vmem_limit_bytes=56 * 2**20
        ),
    )(q, *key_pieces, values)


def project_kernel(n, chunk, att_ref, w_ref, out_ref, w_buf, slots, part, w_sem, send_sem, recv_sem):
    per_owner = out_ref.shape[1] // chunk
    me = lax.axis_index("head")
    up, down = n - 1 - me, me
    both = jnp.minimum(up, down)
    steps = n * per_owner

    def order(u):
        pair = lax.div(u, 2 * per_owner)
        within = lax.rem(u, 2 * per_owner)
        paired_owner = jnp.where(lax.rem(within, 2) == 0, n - 1 - pair, pair)
        single = both + lax.div(jnp.maximum(u - 2 * both * per_owner, 0), per_owner)
        single_owner = jnp.where(up > down, n - 1 - single, single)
        in_pairs = u < 2 * both * per_owner
        owner = jnp.where(in_pairs, paired_owner, single_owner)
        piece = jnp.where(in_pairs, lax.div(within, 2), lax.rem(u, per_owner))
        return jnp.where(u >= steps - per_owner, me, owner), piece

    def load(u):
        owner, piece = order(u)
        panel = owner * per_owner + piece
        columns = pl.ds(pl.multiple_of(panel * chunk, 128), chunk)
        return pltpu.make_async_copy(w_ref.at[:, columns], w_buf.at[panel], w_sem.at[panel]), panel

    def start_load(u, carry):
        load(u)[0].start()
        return carry

    lax.fori_loop(0, steps, start_load, 0)

    barrier = pltpu.get_barrier_semaphore()

    @pl.when(me > 0)
    def _():
        pl.semaphore_signal(barrier, inc=1, device_id={"head": me - 1}, device_id_type=MESH)

    @pl.when(me < n - 1)
    def _():
        pl.semaphore_signal(barrier, inc=1, device_id={"head": me + 1}, device_id_type=MESH)

    ends = (me == 0).astype(jnp.int32) + (me == n - 1).astype(jnp.int32)
    pl.semaphore_wait(barrier, 2 - ends)

    def passed(owner, piece):
        target = jnp.where(owner > me, me + 1, me - 1)
        slot = jnp.where(owner == me - 1, n, owner)
        return pltpu.make_async_remote_copy(
            src_ref=slots.at[owner, piece],
            dst_ref=slots.at[slot, piece],
            send_sem=send_sem.at[owner, piece],
            recv_sem=recv_sem.at[slot, piece],
            device_id={"head": target},
            device_id_type=MESH,
        )

    def arrived(slot, piece, source):
        return pltpu.make_async_remote_copy(
            src_ref=slots.at[slot, piece],
            dst_ref=slots.at[slot, piece],
            send_sem=send_sem.at[slot, piece],
            recv_sem=recv_sem.at[slot, piece],
            device_id={"head": source},
            device_id_type=MESH,
        )

    def one_step(u, carry):
        owner, piece = order(u)
        copy, panel = load(u)
        copy.wait()
        part[...] = dot(att_ref[...], w_buf[panel])

        @pl.when(u < steps - per_owner)
        def _():
            first = jnp.where(owner > me, me == 0, me == n - 1)

            @pl.when(first)
            def _():
                slots[owner, piece] = part[...].astype(BF16)

            @pl.when(jnp.logical_not(first))
            def _():
                arrived(owner, piece, jnp.where(owner > me, me - 1, me + 1)).wait_recv()
                slots[owner, piece] = (part[...] + slots[owner, piece].astype(F32)).astype(BF16)

            passed(owner, piece).start()

        @pl.when(u >= steps - per_owner)
        def _():
            @pl.when(me > 0)
            def _():
                arrived(me, piece, me - 1).wait_recv()
                part[...] += slots[me, piece].astype(F32)

            @pl.when(me < n - 1)
            def _():
                arrived(n, piece, me + 1).wait_recv()
                part[...] += slots[n, piece].astype(F32)

            columns = pl.ds(pl.multiple_of(piece * chunk, 128), chunk)
            out_ref[:, columns] = part[...].astype(BF16)

        return carry

    lax.fori_loop(0, steps, one_step, 0)

    def finish(u, carry):
        passed(*order(u)).wait_send()
        return carry

    lax.fori_loop(0, steps - per_owner, finish, 0)


def project(attended, out_weight):
    n = lax.axis_size("head")
    rows, depth = attended.shape
    columns = out_weight.shape[1] // n
    chunk = math.gcd(columns, 512)
    per_owner = columns // chunk
    in_vmem = pl.BlockSpec(memory_space=pltpu.VMEM)
    return pl.pallas_call(
        functools.partial(project_kernel, n, chunk),
        out_shape=jax.ShapeDtypeStruct((rows, columns), BF16),
        in_specs=[in_vmem, pl.BlockSpec(memory_space=pl.ANY)],
        out_specs=in_vmem,
        scratch_shapes=[
            pltpu.VMEM((n * per_owner, depth, chunk), BF16),
            pltpu.VMEM((n + 1, per_owner, rows, chunk), BF16),
            pltpu.VMEM((rows, chunk), F32),
            pltpu.SemaphoreType.DMA((n * per_owner,)),
            pltpu.SemaphoreType.DMA((n + 1, per_owner)),
            pltpu.SemaphoreType.DMA((n + 1, per_owner)),
        ],
        compiler_params=pltpu.CompilerParams(
            collective_id=2, has_side_effects=True, vmem_limit_bytes=60 * 2**20
        ),
    )(attended, out_weight)


def per_device(hyena_inputs, short_filter, medium_filter, q_proj, k_proj, out_weight):
    hyena_out, key_pieces = filter_block(hyena_inputs, short_filter, medium_filter, k_proj)
    attended = attention(q_proj, key_pieces, hyena_out)
    return (hyena_out, project(attended, out_weight))


def solution(mesh):
    return jax.shard_map(
        per_device,
        mesh=mesh,
        in_specs=(
            P(("batch", "seq"), None, "head"),
            P(None, None, "head"),
            P(None, "head"),
            P(("batch", "seq"), "head"),
            P(("batch", "seq"), "head"),
            P("head", None),
        ),
        out_specs=(P(("batch", "seq"), "head"), P(("batch", "seq"), "head")),
        check_vma=False,
    )
```
